512 devices in a mesh: dp: 32 (over x, z_hi, core), group: 16 (over z_lo, y).
Axes of the slice: x: 4, y: 4, z: 16 (z_hi: 4, z_lo: 4; z = z_hi * 4 + z_lo), core: 2. Of those that a mesh axis runs over, the one named last changes fastest.
Arguments:
- tokens: bfloat16 [2048, 32, 4096], P(('dp', 'group')), may hold values from -40 to 40
- grad_out: bfloat16 [2048, 32, 4096], P(('dp', 'group')), may hold values from -6 to 6
- members: int32 [32, 64], P('dp'), may hold values from 0 to 63, each once within a row
- router: bfloat16 [4096, 1], replicated, may hold values from -1 to 1
- w_in: bfloat16 [1, 4096, 2048], P(None, 'dp', 'group'), may hold values from -0.09375 to 0.09375
- w_out: bfloat16 [1, 2048, 4096], P(None, 'group', 'dp'), may hold values from -0.125 to 0.125
Outputs:
- grad_tokens: bfloat16 [2048, 32, 4096], P(('dp', 'group'))
- grad_w_in: bfloat16 [1, 4096, 2048], P(None, 'dp', 'group')
- grad_w_out: bfloat16 [1, 2048, 4096], P(None, 'group', 'dp')
- grad_router: float32 [4096, 1], replicated
The draws below stay inside these ranges and needn't reach their ends.
Inputs may be any that keep to these rules, and one draw needn't show every extreme that they name: Each row of members holds every number below 64 once.
All inputs are finite; a program needn't handle non-finite values.
Results may differ from the reference program's by a relative error of at most 0.03.
Values may be sent and summed in bfloat16 or wider, within the bound.
No kernel may reach another device: no remote copies, remote signals or barrier semaphores. Data moves between devices by JAX's collectives and lax.ppermute only.
A program may use at most 64 MiB of HBM per device.

```python
import jax
import jax.numpy as jnp
from jax import lax

D = 4096
FF = 2048
EXP = 1
GSIZE = 32
GPOS = 2
LEN = 32
SEQ_ROW = 64
SEQS = 2048
ROWS = 32
N_DP = 32


def router_base(key):
    values = jnp.clip(jax.random.normal(key, (D, EXP), jnp.float32), -6.0, 6.0)
    return values * D ** (-0.5)


def draw_router(key, part):
    shared = router_base(key)
    return shared.astype(jnp.bfloat16)


def draw_tokens(key, part):
    key = jax.random.fold_in(key, 11)
    values = jnp.clip(jax.random.normal(key, (SEQS, LEN, D), jnp.float32), -6.0, 6.0)
    return jnp.clip(values, -40.0, 40.0).astype(jnp.bfloat16)


def shard_levels(stream_key, shape, cuts, smallest, high):
    def one(position, shards_of):
        draws = jax.random.uniform(jax.random.fold_in(jax.random.fold_in(stream_key, 6), position), (shards_of,), jnp.float32, smallest / len(cuts), high / len(cuts))
        return jnp.repeat(jnp.exp(draws), shape[position] // shards_of).reshape((-1,) + (1,) * (len(shape) - position - 1))

    factor_of = one(*cuts[0])
    for cut in cuts[1:]:
        factor_of = factor_of * one(*cut)
    return factor_of


def gaussian(rng, extent, width, reach, cuts=(), kind=jnp.bfloat16):
    array = jax.random.normal(rng, extent, jnp.float32) * width
    if len(cuts) > 0:
        array = shard_levels(rng, extent, cuts, -0.22, 0.18) * array
    return jnp.clip(array, min=-reach, max=reach).astype(kind)


def setup_inputs(seed: int = 0) -> dict:
    key_list = jax.random.split(jax.random.key(seed), 7)
    return {
        "tokens": draw_tokens(jax.random.fold_in(key_list[6], 71), 0),
        "grad_out": gaussian(key_list[1], (SEQS, LEN, D), 1.0, 6.0, ((0, 512),)),
        "members": jax.vmap(lambda own: jax.random.permutation(own, SEQ_ROW))(jax.random.split(key_list[2], ROWS)).reshape((ROWS, SEQ_ROW)).astype(jnp.int32),
        "router": draw_router(jax.random.fold_in(key_list[6], 71), 0),
        "w_in": gaussian(key_list[4], (EXP, D, FF), D ** -0.5, 0.09375, ((1, 32), (2, 16))),
        "w_out": gaussian(key_list[5], (EXP, FF, D), FF ** -0.5, 0.125, ((1, 16), (2, 32))),
    }


def silu_slope(values):
    sigma = jax.nn.sigmoid(values)
    return sigma * (1.0 + values * (1.0 - sigma))


def rounded(values):
    return lax.optimization_barrier(values.astype(jnp.bfloat16)).astype(jnp.float32)


def reference(tokens, grad_out, members, router, w_in, w_out):
    token_all = tokens.reshape(N_DP, SEQ_ROW, LEN, D)
    grad_all = grad_out.reshape(N_DP, SEQ_ROW, LEN, D)
    router_f = router.astype(jnp.float32)
    inner_f = w_in.astype(jnp.float32)
    outer_f = w_out.astype(jnp.float32)

    def one_row(carry, inputs):
        token_row, grad_row, order = inputs
        order = order.astype(jnp.int32)
        token_grp = jnp.take(token_row, order, axis=0).reshape(GPOS, GSIZE, LEN, D).astype(jnp.float32)
        grad_grp = jnp.take(grad_row, order, axis=0).reshape(GPOS, GSIZE, LEN, D).astype(jnp.float32)
        logits = jnp.einsum('kipd,de->kipe', token_grp, router_f)
        weights = jax.nn.softmax(logits, axis=1)
        weights_b = rounded(weights)
        mixed = rounded(jnp.einsum('kipe,kipd->pked', weights_b, token_grp))
        dmix_out = rounded(jnp.einsum('kipe,kipd->pked', weights_b, grad_grp))
        hidden = jnp.einsum('pked,edf->pkef', mixed, inner_f)
        active = rounded(jax.nn.silu(hidden))
        expert_out = rounded(jnp.einsum('pkef,efd->pked', active, outer_f))
        d_act = jnp.einsum('pked,efd->pkef', dmix_out, outer_f)
        d_pre = rounded(d_act * silu_slope(hidden))
        part_out = rounded(jnp.einsum('pkef,pked->efd', active, dmix_out))
        part_in = rounded(jnp.einsum('pked,pkef->edf', mixed, d_pre))
        dmixed = rounded(jnp.einsum('pkef,edf->pked', d_pre, inner_f))
        d_mix = jnp.einsum('kipd,pked->kipe', grad_grp, expert_out) + jnp.einsum('kipd,pked->kipe', token_grp, dmixed)
        centre = jnp.sum(weights * d_mix, axis=1, keepdims=True)
        d_logit = rounded(weights * (d_mix - centre))
        d_tok = jnp.einsum('kipe,pked->kipd', weights_b, dmixed) + jnp.einsum('kipe,de->kipd', d_logit, router_f)
        d_tok = d_tok.astype(jnp.bfloat16).reshape(SEQ_ROW, LEN, D)
        d_route = jnp.einsum('kipd,kipe->de', token_grp, d_logit)
        placed = jnp.zeros((SEQ_ROW, LEN, D), jnp.bfloat16).at[order].set(d_tok)
        acc_in, acc_out, acc_route = carry
        return (acc_in + part_in, acc_out + part_out, acc_route + d_route), placed

    start = (jnp.zeros((EXP, D, FF), jnp.float32), jnp.zeros((EXP, FF, D), jnp.float32), jnp.zeros((D, EXP), jnp.float32))
    totals, placed_all = lax.scan(one_row, start, (token_all, grad_all, members))
    grad_tokens = placed_all.reshape(SEQS, LEN, D)
    return grad_tokens, totals[0].astype(jnp.bfloat16), totals[1].astype(jnp.bfloat16), totals[2]
```

```python
import jax
import jax.numpy as jnp
from jax import lax
from jax.experimental import pallas as pl
from jax.experimental.pallas import tpu as pltpu
from jax.sharding import Mesh, PartitionSpec as P

BF = jnp.bfloat16
F32 = jnp.float32
LOWEST = -1e30
NX, NH, NC, NL, NY = 4, 4, 2, 4, 4
AXES = ("x", "zh", "core", "zl", "y")
HERE, THERE = 32, 32
LIMIT = 32 * 1024 * 1024


def call(body, outs, vmem_args, smem_args=(), flops=0):
    multi = isinstance(outs, (list, tuple))
    arrays = list(smem_args) + list(vmem_args)
    nbytes = sum(a.size * a.dtype.itemsize for a in arrays)
    for o in outs if multi else [outs]:
        nbytes += o.size * o.dtype.itemsize
    vm = pl.BlockSpec(memory_space=pltpu.VMEM)
    sm = pl.BlockSpec(memory_space=pltpu.SMEM)
    return pl.pallas_call(
        body,
        out_shape=outs,
        in_specs=[sm] * len(smem_args) + [vm] * len(vmem_args),
        out_specs=[vm] * len(outs) if multi else vm,
        compiler_params=pltpu.CompilerParams(vmem_limit_bytes=LIMIT),
        cost_estimate=pl.CostEstimate(flops=flops, bytes_accessed=nbytes, transcendentals=0),
    )(*arrays)


def sds(shape, dtype=BF):
    return jax.ShapeDtypeStruct(shape, dtype)


def three(value):
    a = value.astype(BF).astype(F32)
    b = (value - a).astype(BF).astype(F32)
    c = (value - a - b).astype(BF).astype(F32)
    return a, b, c


def pack_stats(top, total):
    lane = lax.broadcasted_iota(jnp.int32, (top.shape[0], 128), 1)
    out = jnp.zeros((top.shape[0], 128), F32)
    for i, term in enumerate(three(top) + three(total)):
        out = jnp.where(lane == i, term, out)
    return out.astype(BF)


def unpack_stats(packed):
    packed = packed.astype(F32)
    lanes = [packed[:, i : i + 1] for i in range(6)]
    return (lanes[0] + lanes[1]) + lanes[2], (lanes[3] + lanes[4]) + lanes[5]


def merge_stats(stats):
    top = stats[0][0]
    for m, _ in stats[1:]:
        top = jnp.maximum(top, m)
    factors = [jnp.exp(m - top) for m, _ in stats]
    total = factors[0] * stats[0][1]
    for f, (_, s) in zip(factors[1:], stats[1:]):
        total = total + f * s
    return top, factors, total


def partial_body(kind, tok, grd, route, out, logit):
    ls = []
    for s in range(4):
        acc = jnp.zeros((32, 512), F32)
        for j in range(8):
            d = slice(j * 512, j * 512 + 512)
            acc = acc + tok[s, :, d].astype(F32) * route[:, d].astype(F32)
        l = jnp.sum(acc, axis=1, keepdims=True)
        ls.append(l)
        logit[s] = jnp.broadcast_to(l, (32, 128))
    tops, sums, weights = [], [], []
    for k in range(2):
        top = jnp.full((32, 1), LOWEST, F32)
        for s in range(4):
            top = jnp.maximum(top, jnp.where(kind[s] == k, ls[s], LOWEST))
        ws = [jnp.where(kind[s] == k, jnp.exp(jnp.minimum(ls[s] - top, 0.0)), 0.0) for s in range(4)]
        tops.append(top)
        sums.append((ws[0] + ws[1]) + (ws[2] + ws[3]))
        weights.append(ws)
    stats = pack_stats(jnp.concatenate(tops, 0), jnp.concatenate(sums, 0))
    for y in range(NY):
        for j in range(4):
            out[y, 128:144, j * 128 : j * 128 + 128] = stats[j * 16 : j * 16 + 16]
        out[y, 128:144, 512:1024] = jnp.zeros((16, 512), BF)
        for h in range(4):
            d = slice(y * 1024 + h * 256, y * 1024 + h * 256 + 256)
            o = slice(h * 256, h * 256 + 256)
            for base, ref in ((0, tok), (64, grd)):
                vals = [ref[s, :, d].astype(F32) for s in range(4)]
                for k in range(2):
                    w = weights[k]
                    acc = (w[0] * vals[0] + w[1] * vals[1]) + (w[2] * vals[2] + w[3] * vals[3])
                    out[y, base + k * 32 : base + k * 32 + 32, o] = acc.astype(BF)


def over_y_body(got, out):
    stats = []
    for i in range(NY):
        rows = [got[i, 128:144, j * 128 : j * 128 + 128] for j in range(4)]
        stats.append(unpack_stats(jnp.concatenate(rows, 0)))
    top, factors, total = merge_stats(stats)
    packed = pack_stats(top, total)
    for z in range(NL):
        for j in range(2):
            out[z, 128:160, j * 128 : j * 128 + 128] = packed[j * 32 : j * 32 + 32]
        for base in (0, 64):
            acc = factors[0] * got[0, base : base + 64, z * 256 : z * 256 + 256].astype(F32)
            for i in range(1, NY):
                acc = acc + factors[i] * got[i, base : base + 64, z * 256 : z * 256 + 256].astype(F32)
            out[z, base : base + 64, :] = acc.astype(BF)


def over_zl_body(got, out, final):
    stats = []
    for i in range(NL):
        rows = [got[i, 128:160, j * 128 : j * 128 + 128] for j in range(2)]
        stats.append(unpack_stats(jnp.concatenate(rows, 0)))
    top, factors, total = merge_stats(stats)
    scale = 1.0 / total
    lane = lax.broadcasted_iota(jnp.int32, (64, 128), 1)
    final[...] = jnp.where(lane == 0, top, total)
    factors = [f * scale for f in factors]
    for base in (0, 64):
        acc = factors[0] * got[0, base : base + 64].astype(F32)
        for i in range(1, NL):
            acc = acc + factors[i] * got[i, base : base + 64].astype(F32)
        acc = acc.astype(BF)
        for z in range(NL):
            out[z, base : base + 64] = acc


def weight_blocks(core, own, other, h, c):
    mine = core == c
    ins = [jnp.where(mine, own[a, h, :128], other[a, h, :128]) for a in range(NX)]
    outs = [jnp.where(mine, own[a, h, 128:], other[a, h, 128:]) for a in range(NX)]
    return jnp.concatenate(ins, 1), jnp.concatenate(outs, 0)


def hidden_body(core, mixed, own, other, out):
    hid = jnp.zeros((64, 512), F32)
    dact = jnp.zeros((64, 512), F32)
    for h in range(NH):
        for c in range(NC):
            win, wout = weight_blocks(core[0], own, other, h, c)
            lanes = slice(c * 128, c * 128 + 128)
            hid = hid + jnp.dot(mixed[h, :64, lanes], win, preferred_element_type=F32)
            dact = dact + lax.dot_general(
                mixed[h, 64:, lanes], wout, (((1,), (1,)), ((), ())), preferred_element_type=F32
            )
    hid = hid.astype(BF)
    dact = dact.astype(BF)
    for y in range(NY):
        out[y, :64] = hid
        out[y, 64:] = dact


def expert_body(core, got, own, other, out, inner):
    hid = got[0, :64].astype(F32)
    dact = got[0, 64:].astype(F32)
    for i in range(1, NY):
        hid = hid + got[i, :64].astype(F32)
        dact = dact + got[i, 64:].astype(F32)
    sigma = jax.nn.sigmoid(hid)
    act = (hid * sigma).astype(BF)
    dpre = (dact * (sigma * (1.0 + hid * (1.0 - sigma)))).astype(BF)
    inner[:64] = act
    inner[64:] = dpre
    for h in range(NH):
        for c in range(NC):
            win, wout = weight_blocks(core[0], own, other, h, c)
            lanes = slice(c * 128, c * 128 + 128)
            out[h, :64, lanes] = jnp.dot(act, wout, preferred_element_type=F32).astype(BF)
            out[h, 64:, lanes] = lax.dot_general(
                dpre, win, (((1,), (1,)), ((), ())), preferred_element_type=F32
            ).astype(BF)


def weight_grad_body(mixed, mixed_other, inner, inner_other, out):
    act = jnp.concatenate([inner[:64], inner_other[:64]], 0)
    dpre = jnp.concatenate([inner[64:], inner_other[64:]], 0)
    for h in range(NH):
        mix = jnp.concatenate([mixed[h, :64], mixed_other[h, :64]], 0)
        dmo = jnp.concatenate([mixed[h, 64:], mixed_other[h, 64:]], 0)
        gin = lax.dot_general(mix, dpre, (((0,), (0,)), ((), ())), preferred_element_type=F32)
        gout = lax.dot_general(act, dmo, (((0,), (0,)), ((), ())), preferred_element_type=F32)
        for a in range(NX):
            out[a, h, :128] = gin[:, a * 128 : a * 128 + 128].astype(BF)
            out[a, h, 128:] = gout[a * 128 : a * 128 + 128].astype(BF)


def sum_four_body(got, out):
    acc = got[0].astype(F32)
    for i in range(1, NL):
        acc = acc + got[i].astype(F32)
    acc = acc.astype(BF)
    for z in range(NL):
        out[z] = acc


def mix_of(kind, logit, final, s):
    rows = pl.ds(pl.multiple_of(kind[s] * 32, 32), 32)
    return jnp.exp(logit[s][:, 0:1] - final[rows, 0:1]) / final[rows, 1:2]


def slope_body(kind, tok, grd, back, logit, final, out, dmix):
    centres = [jnp.zeros((32, 1), F32), jnp.zeros((32, 1), F32)]
    for s in range(4):
        top = pl.multiple_of(kind[s] * 32, 32)
        acc = jnp.zeros((32, 256), F32)
        for y in range(NY):
            for z in range(NL):
                d = slice(y * 1024 + z * 256, y * 1024 + z * 256 + 256)
                eo = back[y, z, pl.ds(top, 32), :].astype(F32)
                dm = back[y, z, pl.ds(top + 64, 32), :].astype(F32)
                acc = acc + (grd[s, :, d].astype(F32) * eo + tok[s, :, d].astype(F32) * dm)
        dm = jnp.sum(acc, axis=1, keepdims=True)
        dmix[s] = jnp.broadcast_to(dm, (32, 128))
        term = mix_of(kind, logit, final, s) * dm
        for k in range(2):
            centres[k] = centres[k] + jnp.where(kind[s] == k, term, 0.0)
    lane = lax.broadcasted_iota(jnp.int32, (8, 128), 1)
    tile = jnp.zeros((8, 128), F32)
    for k in range(2):
        for j in range(4):
            tile = jnp.where(lane == k * 4 + j, centres[k][j * 8 : j * 8 + 8], tile)
    for g in range(NL * NY):
        out[g] = tile


def final_body(kind, tok, back, logit, final, dmix, got, route, dtok, droute):
    tile = got[0]
    for g in range(1, NL * NY):
        tile = tile + got[g]
    centres = [
        jnp.concatenate([tile[:, k * 4 + j : k * 4 + j + 1] for j in range(4)], 0) for k in range(2)
    ]
    mixb, dlogit, tops = [], [], []
    for s in range(4):
        mix = mix_of(kind, logit, final, s)
        centre = jnp.where(kind[s] == 0, centres[0], centres[1])
        dlogit.append((mix * (dmix[s][:, 0:1] - centre)).astype(BF).astype(F32))
        mixb.append(mix.astype(BF).astype(F32))
        tops.append(pl.multiple_of(kind[s] * 32 + 64, 32))
    for y in range(NY):
        for z in range(NL):
            d = slice(y * 1024 + z * 256, y * 1024 + z * 256 + 256)
            r = route[:, d].astype(F32)
            acc = jnp.zeros((32, 256), F32)
            for s in range(4):
                dm = back[y, z, pl.ds(tops[s], 32), :].astype(F32)
                dtok[s, :, d] = (mixb[s] * dm + dlogit[s] * r).astype(BF)
                acc = acc + tok[s, :, d].astype(F32) * dlogit[s]
            total = jnp.sum(acc, axis=0, keepdims=True)
            i = (y * NL + z) // 2
            o = slice((z % 2) * 256, (z % 2) * 256 + 256)
            for g in range(16):
                droute[g, i : i + 1, o] = total


def shards(tokens, grad_out, members, router, w_in, w_out):
    def swap(value, axes):
        return lax.all_to_all(value, axes, split_axis=0, concat_axis=0, tiled=True)

    core = lax.axis_index("core")
    core_s = jnp.full((1,), core, jnp.int32)
    group = lax.axis_index(("zl", "y"))
    flip = [(a * 4 + b, b * 4 + a) for a in range(4) for b in range(4)]
    cores = [(0, 1), (1, 0)]

    shard = jnp.concatenate([w_in[0], w_out[0]], axis=0)
    shard = lax.ppermute(shard, ("x", "y"), flip)
    shard = lax.all_gather(shard, "zh", axis=0, tiled=False)
    shard = swap(jnp.broadcast_to(shard[None], (NX, NH, 256, 128)), "x")
    other = lax.ppermute(shard, "core", cores)

    mine = group * 4 + jnp.arange(4, dtype=jnp.int32)
    kind = jnp.any(members[0, 32:][None, :] == mine[:, None], axis=1).astype(jnp.int32)
    route = router.reshape(1, 4096)

    sent, logit = call(
        partial_body,
        [sds((NY, 144, 1024)), sds((4, 32, 128), F32)],
        (tokens, grad_out, route),
        (kind,),
        flops=10_000_000,
    )
    sent = call(over_y_body, sds((NL, 160, 256)), (swap(sent, "y"),), flops=1_000_000)
    sent, final = call(
        over_zl_body, [sds((NL, 128, 256)), sds((64, 128), F32)], (swap(sent, "zl"),), flops=300_000
    )
    mixed = swap(sent, "zl")
    half = lax.dynamic_slice_in_dim(mixed, (1 - core) * 128, 128, axis=2)
    mixed_half = lax.dynamic_slice_in_dim(mixed, core * 128, 128, axis=2)
    mixed_other = lax.ppermute(half, "core", cores)

    sent = call(hidden_body, sds((NY, 128, 512)), (mixed, shard, other), (core_s,), flops=140_000_000)
    sent, inner = call(
        expert_body,
        [sds((NL, 128, 256)), sds((128, 512))],
        (swap(sent, "y"), shard, other),
        (core_s,),
        flops=140_000_000,
    )
    inner_other = lax.ppermute(inner, "core", cores)
    grads = call(
        weight_grad_body,
        sds((NX, NH, 256, 128)),
        (mixed_half, mixed_other, inner, inner_other),
        flops=140_000_000,
    )
    grads = lax.psum_scatter(grads.reshape(NX * NH * 256, 128), "x", scatter_dimension=0, tiled=True)
    grads = lax.psum_scatter(grads, "zh", scatter_dimension=0, tiled=True)
    grads = lax.ppermute(grads, ("x", "y"), flip)

    sent = call(sum_four_body, sds((NL, 128, 256)), (swap(sent, "zl"),), flops=300_000)
    sent = swap(sent, "zl")
    back = swap(jnp.broadcast_to(sent[None], (NY, NL, 128, 256)), "y")
    sent, dmix = call(
        slope_body,
        [sds((16, 8, 128), F32), sds((4, 32, 128), F32)],
        (tokens, grad_out, back, logit, final),
        (kind,),
        flops=5_000_000,
    )
    grad_tokens, droute = call(
        final_body,
        [sds((4, 32, 4096)), sds((16, 8, 512), F32)],
        (tokens, back, logit, final, dmix, swap(sent, ("zl", "y")), route),
        (kind,),
        flops=5_000_000,
    )
    droute = jnp.sum(swap(droute, ("x", "y")), axis=0)
    droute = jnp.sum(swap(jnp.broadcast_to(droute[None], (16, 8, 512)), ("zh", "zl")), axis=0)
    droute = droute + lax.ppermute(droute, "core", cores)
    return grad_tokens, grads[None, :128], grads[None, 128:], droute.reshape(4096, 1)


def solution(mesh):
    fine = Mesh(mesh.devices.reshape(NX, NH, NC, NL, NY), AXES)
    dp, group = ("x", "zh", "core"), ("zl", "y")
    return jax.shard_map(
        shards,
        mesh=fine,
        in_specs=(
            P(dp + group, None, None),
            P(dp + group, None, None),
            P(dp, None),
            P(),
            P(None, dp, group),
            P(None, group, dp),
        ),
        out_specs=(P(dp + group, None, None), P(None, dp, group), P(None, group, dp), P()),
        check_vma=False,
    )
```

```python
import jax
import jax.numpy as jnp
from jax import lax
from jax.experimental import pallas as pl
from jax.experimental.pallas import tpu as pltpu
from jax.sharding import Mesh, PartitionSpec as P

BF = jnp.bfloat16
F32 = jnp.float32
LOWEST = -1e30
NX, NH, NC, NL, NY = 4, 4, 2, 4, 4
AXES = ("x", "zh", "core", "zl", "y")
HERE, THERE = 32, 32
LIMIT = 32 * 1024 * 1024


def call(body, outs, vmem_args, smem_args=(), flops=0, any_args=(), scratch=()):
    multi = isinstance(outs, (list, tuple))
    arrays = list(smem_args) + list(vmem_args) + list(any_args)
    nbytes = sum(a.size * a.dtype.itemsize for a in arrays)
    for o in outs if multi else [outs]:
        nbytes += o.size * o.dtype.itemsize
    vm = pl.BlockSpec(memory_space=pltpu.VMEM)
    sm = pl.BlockSpec(memory_space=pltpu.SMEM)
    return pl.pallas_call(
        body,
        out_shape=outs,
        in_specs=[sm] * len(smem_args) + [vm] * len(vmem_args) + [pl.BlockSpec(memory_space=pl.ANY)] * len(any_args),
        out_specs=[vm] * len(outs) if multi else vm,
        scratch_shapes=list(scratch),
        compiler_params=pltpu.CompilerParams(vmem_limit_bytes=LIMIT),
        cost_estimate=pl.CostEstimate(flops=flops, bytes_accessed=nbytes, transcendentals=0),
    )(*arrays)


def sds(shape, dtype=BF):
    return jax.ShapeDtypeStruct(shape, dtype)


def three(value):
    a = value.astype(BF).astype(F32)
    b = (value - a).astype(BF).astype(F32)
    c = (value - a - b).astype(BF).astype(F32)
    return a, b, c


def pack_stats(top, total):
    lane = lax.broadcasted_iota(jnp.int32, (top.shape[0], 128), 1)
    out = jnp.zeros((top.shape[0], 128), F32)
    for i, term in enumerate(three(top) + three(total)):
        out = jnp.where(lane == i, term, out)
    return out.astype(BF)


def unpack_stats(packed):
    packed = packed.astype(F32)
    lanes = [packed[:, i : i + 1] for i in range(6)]
    return (lanes[0] + lanes[1]) + lanes[2], (lanes[3] + lanes[4]) + lanes[5]


def merge_stats(stats):
    top = stats[0][0]
    for m, _ in stats[1:]:
        top = jnp.maximum(top, m)
    factors = [jnp.exp(m - top) for m, _ in stats]
    total = factors[0] * stats[0][1]
    for f, (_, s) in zip(factors[1:], stats[1:]):
        total = total + f * s
    return top, factors, total


def partial_body(kind, route, tok_hbm, grd_hbm, out, logit, tok, grd, sems):
    loads = [pltpu.make_async_copy(tok_hbm.at[s], tok.at[s], sems.at[s]) for s in range(4)]
    loads += [pltpu.make_async_copy(grd_hbm.at[s], grd.at[s], sems.at[4 + s]) for s in range(4)]
    for load in loads:
        load.start()
    ls = []
    for s in range(4):
        loads[s].wait()
        acc = jnp.zeros((32, 512), F32)
        for j in range(8):
            d = slice(j * 512, j * 512 + 512)
            acc = acc + tok[s, :, d].astype(F32) * route[:, d].astype(F32)
        l = jnp.sum(acc, axis=1, keepdims=True)
        ls.append(l)
        logit[s] = jnp.broadcast_to(l, (32, 128))
    tops, sums, weights = [], [], []
    for k in range(2):
        top = jnp.full((32, 1), LOWEST, F32)
        for s in range(4):
            top = jnp.maximum(top, jnp.where(kind[s] == k, ls[s], LOWEST))
        ws = [jnp.where(kind[s] == k, jnp.exp(jnp.minimum(ls[s] - top, 0.0)), 0.0) for s in range(4)]
        tops.append(top)
        sums.append((ws[0] + ws[1]) + (ws[2] + ws[3]))
        weights.append(ws)
    stats = pack_stats(jnp.concatenate(tops, 0), jnp.concatenate(sums, 0))
    for s in range(4):
        loads[4 + s].wait()
    for y in range(NY):
        for j in range(4):
            out[y, 128:144, j * 128 : j * 128 + 128] = stats[j * 16 : j * 16 + 16]
        out[y, 128:144, 512:1024] = jnp.zeros((16, 512), BF)
        for h in range(4):
            d = slice(y * 1024 + h * 256, y * 1024 + h * 256 + 256)
            o = slice(h * 256, h * 256 + 256)
            for base, ref in ((0, tok), (64, grd)):
                vals = [ref[s, :, d].astype(F32) for s in range(4)]
                for k in range(2):
                    w = weights[k]
                    acc = (w[0] * vals[0] + w[1] * vals[1]) + (w[2] * vals[2] + w[3] * vals[3])
                    out[y, base + k * 32 : base + k * 32 + 32, o] = acc.astype(BF)


def over_y_body(got, out):
    stats = []
    for i in range(NY):
        rows = [got[i, 128:144, j * 128 : j * 128 + 128] for j in range(4)]
        stats.append(unpack_stats(jnp.concatenate(rows, 0)))
    top, factors, total = merge_stats(stats)
    packed = pack_stats(top, total)
    for z in range(NL):
        for j in range(2):
            out[z, 128:160, j * 128 : j * 128 + 128] = packed[j * 32 : j * 32 + 32]
        for base in (0, 64):
            acc = factors[0] * got[0, base : base + 64, z * 256 : z * 256 + 256].astype(F32)
            for i in range(1, NY):
                acc = acc + factors[i] * got[i, base : base + 64, z * 256 : z * 256 + 256].astype(F32)
            out[z, base : base + 64, :] = acc.astype(BF)


def over_zl_body(got, out, final):
    stats = []
    for i in range(NL):
        rows = [got[i, 128:160, j * 128 : j * 128 + 128] for j in range(2)]
        stats.append(unpack_stats(jnp.concatenate(rows, 0)))
    top, factors, total = merge_stats(stats)
    scale = 1.0 / total
    lane = lax.broadcasted_iota(jnp.int32, (64, 128), 1)
    final[...] = jnp.where(lane == 0, top, total)
    factors = [f * scale for f in factors]
    for base in (0, 64):
        acc = factors[0] * got[0, base : base + 64].astype(F32)
        for i in range(1, NL):
            acc = acc + factors[i] * got[i, base : base + 64].astype(F32)
        acc = acc.astype(BF)
        for z in range(NL):
            out[z, base : base + 64] = acc


def weight_blocks(core, own, other, h, c):
    mine = core == c
    ins = [jnp.where(mine, own[a, h, :128], other[a, h, :128]) for a in range(NX)]
    outs = [jnp.where(mine, own[a, h, 128:], other[a, h, 128:]) for a in range(NX)]
    return jnp.concatenate(ins, 1), jnp.concatenate(outs, 0)


def hidden_body(core, mixed, own, other, out):
    hid = jnp.zeros((64, 512), F32)
    dact = jnp.zeros((64, 512), F32)
    for h in range(NH):
        for c in range(NC):
            win, wout = weight_blocks(core[0], own, other, h, c)
            lanes = slice(c * 128, c * 128 + 128)
            hid = hid + jnp.dot(mixed[h, :64, lanes], win, preferred_element_type=F32)
            dact = dact + lax.dot_general(
                mixed[h, 64:, lanes], wout, (((1,), (1,)), ((), ())), preferred_element_type=F32
            )
    hid = hid.astype(BF)
    dact = dact.astype(BF)
    for y in range(NY):
        out[y, :64] = hid
        out[y, 64:] = dact


def expert_body(core, got, own, other, out, inner):
    hid = got[0, :64].astype(F32)
    dact = got[0, 64:].astype(F32)
    for i in range(1, NY):
        hid = hid + got[i, :64].astype(F32)
        dact = dact + got[i, 64:].astype(F32)
    sigma = jax.nn.sigmoid(hid)
    act = (hid * sigma).astype(BF)
    dpre = (dact * (sigma * (1.0 + hid * (1.0 - sigma)))).astype(BF)
    inner[:64] = act
    inner[64:] = dpre
    for h in range(NH):
        for c in range(NC):
            win, wout = weight_blocks(core[0], own, other, h, c)
            lanes = slice(c * 128, c * 128 + 128)
            out[h, :64, lanes] = jnp.dot(act, wout, preferred_element_type=F32).astype(BF)
            out[h, 64:, lanes] = lax.dot_general(
                dpre, win, (((1,), (1,)), ((), ())), preferred_element_type=F32
            ).astype(BF)


def weight_grad_body(place, mixed, mixed_other, inner, inner_other, out):
    act = jnp.concatenate([inner[:64], inner_other[:64]], 0)
    dpre = jnp.concatenate([inner[64:], inner_other[64:]], 0)
    for h in range(NH):
        mix = jnp.concatenate([mixed[h, :64], mixed_other[h, :64]], 0)
        dmo = jnp.concatenate([mixed[h, 64:], mixed_other[h, 64:]], 0)
        gin = lax.dot_general(mix, dpre, (((0,), (0,)), ((), ())), preferred_element_type=F32)
        gout = lax.dot_general(act, dmo, (((0,), (0,)), ((), ())), preferred_element_type=F32)
        for a in range(NX):
            to = lax.rem(a + NX - place[0], NX)
            out[h, to, :128] = gin[:, a * 128 : a * 128 + 128].astype(BF)
            out[h, to, 128:] = gout[a * 128 : a * 128 + 128].astype(BF)


def sum_four_body(got, out):
    acc = got[0].astype(F32)
    for i in range(1, NL):
        acc = acc + got[i].astype(F32)
    acc = acc.astype(BF)
    for z in range(NL):
        out[z] = acc


def mix_of(kind, logit, final, s):
    rows = pl.ds(pl.multiple_of(kind[s] * 32, 32), 32)
    return jnp.exp(logit[s][:, 0:1] - final[rows, 0:1]) / final[rows, 1:2]


def slope_body(kind, tok, grd, back, logit, final, out, dmix):
    centres = [jnp.zeros((32, 1), F32), jnp.zeros((32, 1), F32)]
    for s in range(4):
        top = pl.multiple_of(kind[s] * 32, 32)
        acc = jnp.zeros((32, 256), F32)
        for y in range(NY):
            for z in range(NL):
                d = slice(y * 1024 + z * 256, y * 1024 + z * 256 + 256)
                eo = back[y, z, pl.ds(top, 32), :].astype(F32)
                dm = back[y, z, pl.ds(top + 64, 32), :].astype(F32)
                acc = acc + (grd[s, :, d].astype(F32) * eo + tok[s, :, d].astype(F32) * dm)
        dm = jnp.sum(acc, axis=1, keepdims=True)
        dmix[s] = jnp.broadcast_to(dm, (32, 128))
        term = mix_of(kind, logit, final, s) * dm
        for k in range(2):
            centres[k] = centres[k] + jnp.where(kind[s] == k, term, 0.0)
    lane = lax.broadcasted_iota(jnp.int32, (8, 128), 1)
    tile = jnp.zeros((8, 128), F32)
    for k in range(2):
        for j in range(4):
            tile = jnp.where(lane == k * 4 + j, centres[k][j * 8 : j * 8 + 8], tile)
    for g in range(NL * NY):
        out[g] = tile


def final_body(kind, tok, back, logit, final, dmix, got, route, dtok, droute):
    tile = got[0]
    for g in range(1, NL * NY):
        tile = tile + got[g]
    centres = [
        jnp.concatenate([tile[:, k * 4 + j : k * 4 + j + 1] for j in range(4)], 0) for k in range(2)
    ]
    mixb, dlogit, tops = [], [], []
    for s in range(4):
        mix = mix_of(kind, logit, final, s)
        centre = jnp.where(kind[s] == 0, centres[0], centres[1])
        dlogit.append((mix * (dmix[s][:, 0:1] - centre)).astype(BF).astype(F32))
        mixb.append(mix.astype(BF).astype(F32))
        tops.append(pl.multiple_of(kind[s] * 32 + 64, 32))
    for y in range(NY):
        for z in range(NL):
            d = slice(y * 1024 + z * 256, y * 1024 + z * 256 + 256)
            r = route[:, d].astype(F32)
            acc = jnp.zeros((32, 256), F32)
            for s in range(4):
                dm = back[y, z, pl.ds(tops[s], 32), :].astype(F32)
                dtok[s, :, d] = (mixb[s] * dm + dlogit[s] * r).astype(BF)
                acc = acc + tok[s, :, d].astype(F32) * dlogit[s]
            total = jnp.sum(acc, axis=0, keepdims=True)
            i = (y * NL + z) // 2
            o = slice((z % 2) * 256, (z % 2) * 256 + 256)
            for g in range(16):
                droute[g, i : i + 1, o] = total


def shards(tokens, grad_out, members, router, w_in, w_out):
    def swap(value, axes):
        return lax.all_to_all(value, axes, split_axis=0, concat_axis=0, tiled=True)

    core = lax.axis_index("core")
    core_s = jnp.full((1,), core, jnp.int32)
    group = lax.axis_index(("zl", "y"))
    flip = [(a * 4 + b, b * 4 + a) for a in range(4) for b in range(4)]
    cores = [(0, 1), (1, 0)]

    mine = group * 4 + jnp.arange(4, dtype=jnp.int32)
    kind = jnp.any(members[0, 32:][None, :] == mine[:, None], axis=1).astype(jnp.int32)
    route = router.reshape(1, 4096)

    sent, logit = call(
        partial_body,
        [sds((NY, 144, 1024)), sds((4, 32, 128), F32)],
        (route,),
        (kind,),
        flops=10_000_000,
        any_args=(tokens, grad_out),
        scratch=(pltpu.VMEM((4, 32, 4096), BF), pltpu.VMEM((4, 32, 4096), BF), pltpu.SemaphoreType.DMA((8,))),
    )
    shard = jnp.concatenate([w_in[0], w_out[0]], axis=0)
    shard = lax.ppermute(shard, ("x", "y"), flip)
    sent, shard = lax.optimization_barrier((sent, shard))
    shard = lax.all_gather(shard, "zh", axis=0, tiled=False)
    shard = swap(jnp.broadcast_to(shard[None], (NX, NH, 256, 128)), "x")
    other = lax.ppermute(shard, "core", cores)

    sent = call(over_y_body, sds((NL, 160, 256)), (swap(sent, "y"),), flops=1_000_000)
    sent, final = call(
        over_zl_body, [sds((NL, 128, 256)), sds((64, 128), F32)], (swap(sent, "zl"),), flops=300_000
    )
    mixed = swap(sent, "zl")
    half = lax.dynamic_slice_in_dim(mixed, (1 - core) * 128, 128, axis=2)
    mixed_half = lax.dynamic_slice_in_dim(mixed, core * 128, 128, axis=2)
    mixed_other = lax.ppermute(half, "core", cores)

    sent = call(hidden_body, sds((NY, 128, 512)), (mixed, shard, other), (core_s,), flops=140_000_000)
    got, mixed_other = lax.optimization_barrier((swap(sent, "y"), mixed_other))
    sent, inner = call(
        expert_body,
        [sds((NL, 128, 256)), sds((128, 512))],
        (got, shard, other),
        (core_s,),
        flops=140_000_000,
    )
    inner_other = lax.ppermute(inner, "core", cores)
    grads = call(
        weight_grad_body,
        sds((NX, NH, 256, 128)),
        (mixed_half, mixed_other, inner, inner_other),
        (jnp.full((1,), lax.axis_index("x"), jnp.int32),),
        flops=140_000_000,
    )
    got, grads = lax.optimization_barrier((swap(sent, "zl"), grads))
    grads = lax.psum_scatter(grads.reshape(NX * NH * 256, 128), "zh", scatter_dimension=0, tiled=True)

    sent = call(sum_four_body, sds((NL, 128, 256)), (got,), flops=300_000)
    sent = swap(sent, "zl")
    back = swap(jnp.broadcast_to(sent[None], (NY, NL, 128, 256)), "y")
    sent, dmix = call(
        slope_body,
        [sds((16, 8, 128), F32), sds((4, 32, 128), F32)],
        (tokens, grad_out, back, logit, final),
        (kind,),
        flops=5_000_000,
    )
    grad_tokens, droute = call(
        final_body,
        [sds((4, 32, 4096)), sds((16, 8, 512), F32)],
        (tokens, back, logit, final, dmix, swap(sent, ("zl", "y")), route),
        (kind,),
        flops=5_000_000,
    )
    droute, grads = lax.optimization_barrier((swap(droute, ("x", "y")), grads))
    droute = jnp.sum(droute, axis=0)
    droute = swap(jnp.broadcast_to(droute[None], (16, 8, 512)), ("zh", "zl"))
    grads = grads.reshape(NX, 256, 128)
    parts = [
        lax.ppermute(
            grads[i], ("x", "y"), [(x * NY + y, y * NY + (x + i) % NX) for x in range(NX) for y in range(NY)]
        )
        for i in range(NX)
    ]
    droute, parts = lax.optimization_barrier((droute, parts))
    parts = [p.astype(F32) for p in parts]
    grads = ((parts[0] + parts[1]) + (parts[2] + parts[3])).astype(BF)
    droute = jnp.sum(droute, axis=0)
    droute = droute + lax.ppermute(droute, "core", cores)
    return grad_tokens, grads[None, :128], grads[None, 128:], droute.reshape(4096, 1)


def solution(mesh):
    fine = Mesh(mesh.devices.reshape(NX, NH, NC, NL, NY), AXES)
    dp, group = ("x", "zh", "core"), ("zl", "y")
    return jax.shard_map(
        shards,
        mesh=fine,
        in_specs=(
            P(dp + group, None, None),
            P(dp + group, None, None),
            P(dp, None),
            P(),
            P(None, dp, group),
            P(None, group, dp),
        ),
        out_specs=(P(dp + group, None, None), P(None, dp, group), P(None, group, dp), P()),
        check_vma=False,
    )
```

```python
import jax
import jax.numpy as jnp
from jax import lax
from jax.experimental import pallas as pl
from jax.experimental.pallas import tpu as pltpu
from jax.sharding import Mesh, PartitionSpec as P

BF = jnp.bfloat16
F32 = jnp.float32
LOWEST = -1e30
NX, NH, NC, NL, NY = 4, 4, 2, 4, 4
AXES = ("x", "zh", "core", "zl", "y")
HERE, THERE = 32, 32
LIMIT = 32 * 1024 * 1024


def call(body, outs, vmem_args, smem_args=(), flops=0, any_args=(), scratch=(), limit=LIMIT):
    multi = isinstance(outs, (list, tuple))
    arrays = list(smem_args) + list(vmem_args) + list(any_args)
    nbytes = sum(a.size * a.dtype.itemsize for a in arrays)
    for o in outs if multi else [outs]:
        nbytes += o.size * o.dtype.itemsize
    vm = pl.BlockSpec(memory_space=pltpu.VMEM)
    sm = pl.BlockSpec(memory_space=pltpu.SMEM)
    return pl.pallas_call(
        body,
        out_shape=outs,
        in_specs=[sm] * len(smem_args) + [vm] * len(vmem_args) + [pl.BlockSpec(memory_space=pl.ANY)] * len(any_args),
        out_specs=[sm if o.dtype == jnp.int32 else vm for o in outs] if multi else vm,
        scratch_shapes=list(scratch),
        compiler_params=pltpu.CompilerParams(vmem_limit_bytes=limit),
        cost_estimate=pl.CostEstimate(flops=flops, bytes_accessed=nbytes, transcendentals=0),
    )(*arrays)


def sds(shape, dtype=BF):
    return jax.ShapeDtypeStruct(shape, dtype)


def three(value):
    a = value.astype(BF).astype(F32)
    b = (value - a).astype(BF).astype(F32)
    c = (value - a - b).astype(BF).astype(F32)
    return a, b, c


def pack_stats(top, total):
    lane = lax.broadcasted_iota(jnp.int32, (top.shape[0], 128), 1)
    out = jnp.zeros((top.shape[0], 128), F32)
    for i, term in enumerate(three(top) + three(total)):
        out = jnp.where(lane == i, term, out)
    return out.astype(BF)


def unpack_stats(packed):
    packed = packed.astype(F32)
    lanes = [packed[:, i : i + 1] for i in range(6)]
    return (lanes[0] + lanes[1]) + lanes[2], (lanes[3] + lanes[4]) + lanes[5]


def merge_stats(stats):
    top = stats[0][0]
    for m, _ in stats[1:]:
        top = jnp.maximum(top, m)
    factors = [jnp.exp(m - top) for m, _ in stats]
    total = factors[0] * stats[0][1]
    for f, (_, s) in zip(factors[1:], stats[1:]):
        total = total + f * s
    return top, factors, total


def partial_body(first, order, route, tok_hbm, grd_hbm, out, logit, kind_out, tok, grd, sems):
    loads = [pltpu.make_async_copy(tok_hbm.at[s], tok.at[s], sems.at[s]) for s in range(4)]
    loads += [pltpu.make_async_copy(grd_hbm.at[s], grd.at[s], sems.at[4 + s]) for s in range(4)]
    for load in loads:
        load.start()
    kind = []
    for s in range(4):
        hits = jnp.int32(0)
        for j in range(32, 64):
            hits = hits + (order[0, j] == first[0] + s).astype(jnp.int32)
        kind_out[s] = hits
        kind.append(hits)
    ls = []
    for s in range(4):
        loads[s].wait()
        acc = jnp.zeros((32, 512), F32)
        for j in range(8):
            d = slice(j * 512, j * 512 + 512)
            acc = acc + tok[s, :, d].astype(F32) * route[:, d].astype(F32)
        l = jnp.sum(acc, axis=1, keepdims=True)
        ls.append(l)
        logit[s] = jnp.broadcast_to(l, (32, 128))
    tops, sums, weights = [], [], []
    for k in range(2):
        top = jnp.full((32, 1), LOWEST, F32)
        for s in range(4):
            top = jnp.maximum(top, jnp.where(kind[s] == k, ls[s], LOWEST))
        ws = [jnp.where(kind[s] == k, jnp.exp(jnp.minimum(ls[s] - top, 0.0)), 0.0) for s in range(4)]
        tops.append(top)
        sums.append((ws[0] + ws[1]) + (ws[2] + ws[3]))
        weights.append(ws)
    stats = pack_stats(jnp.concatenate(tops, 0), jnp.concatenate(sums, 0))
    for s in range(4):
        loads[4 + s].wait()
    for y in range(NY):
        for j in range(4):
            out[y, 128:144, j * 128 : j * 128 + 128] = stats[j * 16 : j * 16 + 16]
        out[y, 128:144, 512:1024] = jnp.zeros((16, 512), BF)
        for h in range(4):
            d = slice(y * 1024 + h * 256, y * 1024 + h * 256 + 256)
            o = slice(h * 256, h * 256 + 256)
            for base, ref in ((0, tok), (64, grd)):
                vals = [ref[s, :, d].astype(F32) for s in range(4)]
                for k in range(2):
                    w = weights[k]
                    acc = (w[0] * vals[0] + w[1] * vals[1]) + (w[2] * vals[2] + w[3] * vals[3])
                    out[y, base + k * 32 : base + k * 32 + 32, o] = acc.astype(BF)


def over_y_body(got, out):
    stats = []
    for i in range(NY):
        rows = [got[i, 128:144, j * 128 : j * 128 + 128] for j in range(4)]
        stats.append(unpack_stats(jnp.concatenate(rows, 0)))
    top, factors, total = merge_stats(stats)
    packed = pack_stats(top, total)
    for z in range(NL):
        for j in range(2):
            out[z, 128:160, j * 128 : j * 128 + 128] = packed[j * 32 : j * 32 + 32]
        for base in (0, 64):
            acc = factors[0] * got[0, base : base + 64, z * 256 : z * 256 + 256].astype(F32)
            for i in range(1, NY):
                acc = acc + factors[i] * got[i, base : base + 64, z * 256 : z * 256 + 256].astype(F32)
            out[z, base : base + 64, :] = acc.astype(BF)


def over_zl_body(got, out, final):
    stats = []
    for i in range(NL):
        rows = [got[i, 128:160, j * 128 : j * 128 + 128] for j in range(2)]
        stats.append(unpack_stats(jnp.concatenate(rows, 0)))
    top, factors, total = merge_stats(stats)
    scale = 1.0 / total
    lane = lax.broadcasted_iota(jnp.int32, (64, 128), 1)
    final[...] = jnp.where(lane == 0, top, total)
    factors = [f * scale for f in factors]
    for base in (0, 64):
        acc = factors[0] * got[0, base : base + 64].astype(F32)
        for i in range(1, NL):
            acc = acc + factors[i] * got[i, base : base + 64].astype(F32)
        acc = acc.astype(BF)
        for z in range(NL):
            out[z, base : base + 64] = acc


def weight_blocks(core, own, other, h, c):
    mine = core == c
    ins = [jnp.where(mine, own[a, h, :128], other[a, h, :128]) for a in range(NX)]
    outs = [jnp.where(mine, own[a, h, 128:], other[a, h, 128:]) for a in range(NX)]
    return jnp.concatenate(ins, 1), jnp.concatenate(outs, 0)


def hidden_body(core, mixed, own, other, out):
    hid = jnp.zeros((64, 512), F32)
    dact = jnp.zeros((64, 512), F32)
    for h in range(NH):
        for c in range(NC):
            win, wout = weight_blocks(core[0], own, other, h, c)
            lanes = slice(c * 128, c * 128 + 128)
            hid = hid + jnp.dot(mixed[h, :64, lanes], win, preferred_element_type=F32)
            dact = dact + lax.dot_general(
                mixed[h, 64:, lanes], wout, (((1,), (1,)), ((), ())), preferred_element_type=F32
            )
    hid = hid.astype(BF)
    dact = dact.astype(BF)
    for y in range(NY):
        out[y, :64] = hid
        out[y, 64:] = dact


def expert_body(core, got, own, other, out, inner):
    hid = got[0, :64].astype(F32)
    dact = got[0, 64:].astype(F32)
    for i in range(1, NY):
        hid = hid + got[i, :64].astype(F32)
        dact = dact + got[i, 64:].astype(F32)
    sigma = jax.nn.sigmoid(hid)
    act = (hid * sigma).astype(BF)
    dpre = (dact * (sigma * (1.0 + hid * (1.0 - sigma)))).astype(BF)
    inner[:64] = act
    inner[64:] = dpre
    for h in range(NH):
        for c in range(NC):
            win, wout = weight_blocks(core[0], own, other, h, c)
            lanes = slice(c * 128, c * 128 + 128)
            out[h, :64, lanes] = jnp.dot(act, wout, preferred_element_type=F32).astype(BF)
            out[h, 64:, lanes] = lax.dot_general(
                dpre, win, (((1,), (1,)), ((), ())), preferred_element_type=F32
            ).astype(BF)


def weight_grad_body(mixed, mixed_other, inner, inner_other, out):
    act = jnp.concatenate([inner[:64], inner_other[:64]], 0)
    dpre = jnp.concatenate([inner[64:], inner_other[64:]], 0)
    for h in range(NH):
        mix = jnp.concatenate([mixed[h, :64], mixed_other[h, :64]], 0)
        dmo = jnp.concatenate([mixed[h, 64:], mixed_other[h, 64:]], 0)
        gin = lax.dot_general(mix, dpre, (((0,), (0,)), ((), ())), preferred_element_type=F32)
        gout = lax.dot_general(act, dmo, (((0,), (0,)), ((), ())), preferred_element_type=F32)
        for a in range(NX):
            out[a, h, :128] = gin[:, a * 128 : a * 128 + 128].astype(BF)
            out[a, h, 128:] = gout[a * 128 : a * 128 + 128].astype(BF)


def sum_four_body(got, out):
    acc = got[0].astype(F32)
    for i in range(1, NL):
        acc = acc + got[i].astype(F32)
    acc = acc.astype(BF)
    for z in range(NL):
        out[z] = acc


def mix_of(kind, logit, final, s):
    rows = pl.ds(pl.multiple_of(kind[s] * 32, 32), 32)
    return jnp.exp(logit[s][:, 0:1] - final[rows, 0:1]) / final[rows, 1:2]


def slope_body(kind, tok, grd, back, logit, final, out, dmix):
    centres = [jnp.zeros((32, 1), F32), jnp.zeros((32, 1), F32)]
    for s in range(4):
        top = pl.multiple_of(kind[s] * 32, 32)
        acc = jnp.zeros((32, 256), F32)
        for y in range(NY):
            for z in range(NL):
                d = slice(y * 1024 + z * 256, y * 1024 + z * 256 + 256)
                eo = back[y, z, pl.ds(top, 32), :].astype(F32)
                dm = back[y, z, pl.ds(top + 64, 32), :].astype(F32)
                acc = acc + (grd[s, :, d].astype(F32) * eo + tok[s, :, d].astype(F32) * dm)
        dm = jnp.sum(acc, axis=1, keepdims=True)
        dmix[s] = jnp.broadcast_to(dm, (32, 128))
        term = mix_of(kind, logit, final, s) * dm
        for k in range(2):
            centres[k] = centres[k] + jnp.where(kind[s] == k, term, 0.0)
    lane = lax.broadcasted_iota(jnp.int32, (8, 128), 1)
    tile = jnp.zeros((8, 128), F32)
    for k in range(2):
        for j in range(4):
            tile = jnp.where(lane == k * 4 + j, centres[k][j * 8 : j * 8 + 8], tile)
    for g in range(NL * NY):
        out[g] = tile


def final_body(kind, tok, back, logit, final, dmix, got, route, dtok, droute):
    tile = got[0]
    for g in range(1, NL * NY):
        tile = tile + got[g]
    centres = [
        jnp.concatenate([tile[:, k * 4 + j : k * 4 + j + 1] for j in range(4)], 0) for k in range(2)
    ]
    mixb, dlogit, tops = [], [], []
    for s in range(4):
        mix = mix_of(kind, logit, final, s)
        centre = jnp.where(kind[s] == 0, centres[0], centres[1])
        dlogit.append((mix * (dmix[s][:, 0:1] - centre)).astype(BF).astype(F32))
        mixb.append(mix.astype(BF).astype(F32))
        tops.append(pl.multiple_of(kind[s] * 32 + 64, 32))
    for y in range(NY):
        for z in range(NL):
            d = slice(y * 1024 + z * 256, y * 1024 + z * 256 + 256)
            r = route[:, d].astype(F32)
            acc = jnp.zeros((32, 256), F32)
            for s in range(4):
                dm = back[y, z, pl.ds(tops[s], 32), :].astype(F32)
                dtok[s, :, d] = (mixb[s] * dm + dlogit[s] * r).astype(BF)
                acc = acc + tok[s, :, d].astype(F32) * dlogit[s]
            total = jnp.sum(acc, axis=0, keepdims=True)
            i = (y * NL + z) // 2
            o = slice((z % 2) * 256, (z % 2) * 256 + 256)
            for g in range(16):
                droute[g, i : i + 1, o] = total


def shards(tokens, grad_out, members, router, w_in, w_out):
    def swap(value, axes):
        return lax.all_to_all(value, axes, split_axis=0, concat_axis=0, tiled=True)

    core = lax.axis_index("core")
    core_s = jnp.full((1,), core, jnp.int32)
    group = lax.axis_index(("zl", "y"))
    flip = [(a * 4 + b, b * 4 + a) for a in range(4) for b in range(4)]
    cores = [(0, 1), (1, 0)]

    route = router.reshape(1, 4096)

    sent, logit, kind = call(
        partial_body,
        [sds((NY, 144, 1024)), sds((4, 32, 128), F32), sds((4,), jnp.int32)],
        (route,),
        (jnp.full((1,), group * 4, jnp.int32), members),
        flops=10_000_000,
        any_args=(tokens, grad_out),
        scratch=(pltpu.VMEM((4, 32, 4096), BF), pltpu.VMEM((4, 32, 4096), BF), pltpu.SemaphoreType.DMA((8,))),
        limit=63 * 1024 * 1024,
    )
    shard = jnp.concatenate([w_in[0], w_out[0]], axis=0)
    shard = lax.ppermute(shard, ("x", "y"), flip)
    sent, shard = lax.optimization_barrier((sent, shard))
    shard = lax.all_gather(shard, "zh", axis=0, tiled=False)
    shard = swap(jnp.broadcast_to(shard[None], (NX, NH, 256, 128)), "x")
    other = lax.ppermute(shard, "core", cores)

    sent = call(over_y_body, sds((NL, 160, 256)), (swap(sent, "y"),), flops=1_000_000)
    sent, final = call(
        over_zl_body, [sds((NL, 128, 256)), sds((64, 128), F32)], (swap(sent, "zl"),), flops=300_000
    )
    mixed = swap(sent, "zl")
    half = lax.dynamic_slice_in_dim(mixed, (1 - core) * 128, 128, axis=2)
    mixed_half = lax.dynamic_slice_in_dim(mixed, core * 128, 128, axis=2)
    mixed_other = lax.ppermute(half, "core", cores)

    sent = call(hidden_body, sds((NY, 128, 512)), (mixed, shard, other), (core_s,), flops=140_000_000)
    got, mixed_other = lax.optimization_barrier((swap(sent, "y"), mixed_other))
    sent, inner = call(
        expert_body,
        [sds((NL, 128, 256)), sds((128, 512))],
        (got, shard, other),
        (core_s,),
        flops=140_000_000,
    )
    inner_other = lax.ppermute(inner, "core", cores)
    grads = call(
        weight_grad_body,
        sds((NX, NH, 256, 128)),
        (mixed_half, mixed_other, inner, inner_other),
        flops=140_000_000,
    )
    got, grads = lax.optimization_barrier((swap(sent, "zl"), grads))
    grads = lax.psum_scatter(grads.reshape(NX * NH * 256, 128), "x", scatter_dimension=0, tiled=True)

    sent = call(sum_four_body, sds((NL, 128, 256)), (got,), flops=300_000)
    sent = swap(sent, "zl")
    back = swap(jnp.broadcast_to(sent[None], (NY, NL, 128, 256)), "y")
    sent, dmix = call(
        slope_body,
        [sds((16, 8, 128), F32), sds((4, 32, 128), F32)],
        (tokens, grad_out, back, logit, final),
        (kind,),
        flops=5_000_000,
    )
    sent, grads = lax.optimization_barrier((sent, grads))
    grads = lax.psum_scatter(grads, "zh", scatter_dimension=0, tiled=True)
    grad_tokens, droute = call(
        final_body,
        [sds((4, 32, 4096)), sds((16, 8, 512), F32)],
        (tokens, back, logit, final, dmix, swap(sent, ("zl", "y")), route),
        (kind,),
        flops=5_000_000,
    )
    droute = jnp.sum(swap(droute, ("x", "y")), axis=0)
    droute = droute + lax.ppermute(droute, "core", cores)
    droute, grads = lax.optimization_barrier((droute, grads))
    droute = swap(jnp.broadcast_to(droute[None], (16, 8, 512)), ("zh", "zl"))
    grads = lax.ppermute(grads, ("x", "y"), flip)
    droute, grads = lax.optimization_barrier((droute, grads))
    droute = jnp.sum(droute, axis=0)
    return grad_tokens, grads[None, :128], grads[None, 128:], droute.reshape(4096, 1)


def solution(mesh):
    fine = Mesh(mesh.devices.reshape(NX, NH, NC, NL, NY), AXES)
    dp, group = ("x", "zh", "core"), ("zl", "y")
    return jax.shard_map(
        shards,
        mesh=fine,
        in_specs=(
            P(dp + group, None, None),
            P(dp + group, None, None),
            P(dp, None),
            P(),
            P(None, dp, group),
            P(None, group, dp),
        ),
        out_specs=(P(dp + group, None, None), P(None, dp, group), P(None, group, dp), P()),
        check_vma=False,
    )
```

```python
import jax
import jax.numpy as jnp
from jax import lax
from jax.experimental import pallas as pl
from jax.experimental.pallas import tpu as pltpu
from jax.sharding import Mesh, PartitionSpec as P

BF = jnp.bfloat16
F32 = jnp.float32
LOWEST = -1e30
NX, NH, NC, NL, NY = 4, 4, 2, 4, 4
AXES = ("x", "zh", "core", "zl", "y")
HERE, THERE = 32, 32
LIMIT = 32 * 1024 * 1024


def call(body, outs, vmem_args, smem_args=(), flops=0, any_args=(), scratch=(), limit=LIMIT):
    multi = isinstance(outs, (list, tuple))
    arrays = list(smem_args) + list(vmem_args) + list(any_args)
    nbytes = sum(a.size * a.dtype.itemsize for a in arrays)
    for o in outs if multi else [outs]:
        nbytes += o.size * o.dtype.itemsize
    vm = pl.BlockSpec(memory_space=pltpu.VMEM)
    sm = pl.BlockSpec(memory_space=pltpu.SMEM)
    return pl.pallas_call(
        body,
        out_shape=outs,
        in_specs=[sm] * len(smem_args) + [vm] * len(vmem_args) + [pl.BlockSpec(memory_space=pl.ANY)] * len(any_args),
        out_specs=[sm if o.dtype == jnp.int32 else vm for o in outs] if multi else vm,
        scratch_shapes=list(scratch),
        compiler_params=pltpu.CompilerParams(vmem_limit_bytes=limit),
        cost_estimate=pl.CostEstimate(flops=flops, bytes_accessed=nbytes, transcendentals=0),
    )(*arrays)


def sds(shape, dtype=BF):
    return jax.ShapeDtypeStruct(shape, dtype)


def three(value):
    a = value.astype(BF).astype(F32)
    b = (value - a).astype(BF).astype(F32)
    c = (value - a - b).astype(BF).astype(F32)
    return a, b, c


def pack_stats(top, total):
    lane = lax.broadcasted_iota(jnp.int32, (top.shape[0], 128), 1)
    out = jnp.zeros((top.shape[0], 128), F32)
    for i, term in enumerate(three(top) + three(total)):
        out = jnp.where(lane == i, term, out)
    return out.astype(BF)


def unpack_stats(packed):
    packed = packed.astype(F32)
    lanes = [packed[:, i : i + 1] for i in range(6)]
    return (lanes[0] + lanes[1]) + lanes[2], (lanes[3] + lanes[4]) + lanes[5]


def merge_stats(stats):
    top = stats[0][0]
    for m, _ in stats[1:]:
        top = jnp.maximum(top, m)
    factors = [jnp.exp(m - top) for m, _ in stats]
    total = factors[0] * stats[0][1]
    for f, (_, s) in zip(factors[1:], stats[1:]):
        total = total + f * s
    return top, factors, total


def partial_body(first, order, route, tok_hbm, grd_hbm, out, logit, kind_out, tok, grd, sems):
    loads = [pltpu.make_async_copy(tok_hbm.at[s], tok.at[s], sems.at[s]) for s in range(4)]
    loads += [pltpu.make_async_copy(grd_hbm.at[s], grd.at[s], sems.at[4 + s]) for s in range(4)]
    for load in loads:
        load.start()
    kind = []
    for s in range(4):
        hits = jnp.int32(0)
        for j in range(32, 64):
            hits = hits + (order[0, j] == first[0] + s).astype(jnp.int32)
        kind_out[s] = hits
        kind.append(hits)
    ls = []
    for s in range(4):
        loads[s].wait()
        acc = jnp.zeros((32, 512), F32)
        for j in range(8):
            d = slice(j * 512, j * 512 + 512)
            acc = acc + tok[s, :, d].astype(F32) * route[:, d].astype(F32)
        l = jnp.sum(acc, axis=1, keepdims=True)
        ls.append(l)
        logit[s] = jnp.broadcast_to(l, (32, 128))
    tops, sums, weights = [], [], []
    for k in range(2):
        top = jnp.full((32, 1), LOWEST, F32)
        for s in range(4):
            top = jnp.maximum(top, jnp.where(kind[s] == k, ls[s], LOWEST))
        ws = [jnp.where(kind[s] == k, jnp.exp(jnp.minimum(ls[s] - top, 0.0)), 0.0) for s in range(4)]
        tops.append(top)
        sums.append((ws[0] + ws[1]) + (ws[2] + ws[3]))
        weights.append(ws)
    stats = pack_stats(jnp.concatenate(tops, 0), jnp.concatenate(sums, 0))
    for s in range(4):
        loads[4 + s].wait()
    for y in range(NY):
        for j in range(4):
            out[y, 128:144, j * 128 : j * 128 + 128] = stats[j * 16 : j * 16 + 16]
        out[y, 128:144, 512:1024] = jnp.zeros((16, 512), BF)
        for h in range(4):
            d = slice(y * 1024 + h * 256, y * 1024 + h * 256 + 256)
            o = slice(h * 256, h * 256 + 256)
            for base, ref in ((0, tok), (64, grd)):
                vals = [ref[s, :, d].astype(F32) for s in range(4)]
                for k in range(2):
                    w = weights[k]
                    acc = (w[0] * vals[0] + w[1] * vals[1]) + (w[2] * vals[2] + w[3] * vals[3])
                    out[y, base + k * 32 : base + k * 32 + 32, o] = acc.astype(BF)


def over_y_body(at, got, *outs):
    stats = []
    for i in range(NY):
        rows = [got[i, 128:144, j * 128 : j * 128 + 128] for j in range(4)]
        stats.append(unpack_stats(jnp.concatenate(rows, 0)))
    top, factors, total = merge_stats(stats)
    packed = pack_stats(top, total)
    for step, out in enumerate(outs):
        d = pl.ds(pl.multiple_of(lax.rem(at[0] + step, NL) * 256, 256), 256)
        for j in range(2):
            out[128:160, j * 128 : j * 128 + 128] = packed[j * 32 : j * 32 + 32]
        for base in (0, 64):
            acc = factors[0] * got[0, base : base + 64, d].astype(F32)
            for i in range(1, NY):
                acc = acc + factors[i] * got[i, base : base + 64, d].astype(F32)
            out[base : base + 64, :] = acc.astype(BF)


def over_zl_body(*refs):
    got, out, final = refs[:NL], refs[NL], refs[NL + 1]
    stats = []
    for i in range(NL):
        rows = [got[i][128:160, j * 128 : j * 128 + 128] for j in range(2)]
        stats.append(unpack_stats(jnp.concatenate(rows, 0)))
    top, factors, total = merge_stats(stats)
    scale = 1.0 / total
    lane = lax.broadcasted_iota(jnp.int32, (64, 128), 1)
    final[...] = jnp.where(lane == 0, top, total)
    factors = [f * scale for f in factors]
    for base in (0, 64):
        acc = factors[0] * got[0][base : base + 64].astype(F32)
        for i in range(1, NL):
            acc = acc + factors[i] * got[i][base : base + 64].astype(F32)
        acc = acc.astype(BF)
        for z in range(NL):
            out[z, base : base + 64] = acc


def weight_blocks(core, own, other, h, c):
    mine = core == c
    ins = [jnp.where(mine, own[a, h, :128], other[a, h, :128]) for a in range(NX)]
    outs = [jnp.where(mine, own[a, h, 128:], other[a, h, 128:]) for a in range(NX)]
    return jnp.concatenate(ins, 1), jnp.concatenate(outs, 0)


def hidden_body(core, mixed, own, other, out):
    hid = jnp.zeros((64, 512), F32)
    dact = jnp.zeros((64, 512), F32)
    for h in range(NH):
        for c in range(NC):
            win, wout = weight_blocks(core[0], own, other, h, c)
            lanes = slice(c * 128, c * 128 + 128)
            hid = hid + jnp.dot(mixed[h, :64, lanes], win, preferred_element_type=F32)
            dact = dact + lax.dot_general(
                mixed[h, 64:, lanes], wout, (((1,), (1,)), ((), ())), preferred_element_type=F32
            )
    hid = hid.astype(BF)
    dact = dact.astype(BF)
    for y in range(NY):
        out[y, :64] = hid
        out[y, 64:] = dact


def expert_body(core, got, own, other, out, inner):
    hid = got[0, :64].astype(F32)
    dact = got[0, 64:].astype(F32)
    for i in range(1, NY):
        hid = hid + got[i, :64].astype(F32)
        dact = dact + got[i, 64:].astype(F32)
    sigma = jax.nn.sigmoid(hid)
    act = (hid * sigma).astype(BF)
    dpre = (dact * (sigma * (1.0 + hid * (1.0 - sigma)))).astype(BF)
    inner[:64] = act
    inner[64:] = dpre
    for h in range(NH):
        for c in range(NC):
            win, wout = weight_blocks(core[0], own, other, h, c)
            lanes = slice(c * 128, c * 128 + 128)
            out[h, :64, lanes] = jnp.dot(act, wout, preferred_element_type=F32).astype(BF)
            out[h, 64:, lanes] = lax.dot_general(
                dpre, win, (((1,), (1,)), ((), ())), preferred_element_type=F32
            ).astype(BF)


def weight_grad_body(mixed, mixed_other, inner, inner_other, out):
    act = jnp.concatenate([inner[:64], inner_other[:64]], 0)
    dpre = jnp.concatenate([inner[64:], inner_other[64:]], 0)
    for h in range(NH):
        mix = jnp.concatenate([mixed[h, :64], mixed_other[h, :64]], 0)
        dmo = jnp.concatenate([mixed[h, 64:], mixed_other[h, 64:]], 0)
        gin = lax.dot_general(mix, dpre, (((0,), (0,)), ((), ())), preferred_element_type=F32)
        gout = lax.dot_general(act, dmo, (((0,), (0,)), ((), ())), preferred_element_type=F32)
        for a in range(NX):
            out[a, h, :128] = gin[:, a * 128 : a * 128 + 128].astype(BF)
            out[a, h, 128:] = gout[a * 128 : a * 128 + 128].astype(BF)


def sum_four_body(got, out):
    acc = got[0].astype(F32)
    for i in range(1, NL):
        acc = acc + got[i].astype(F32)
    acc = acc.astype(BF)
    for z in range(NL):
        out[z] = acc


def mix_of(kind, logit, final, s):
    rows = pl.ds(pl.multiple_of(kind[s] * 32, 32), 32)
    return jnp.exp(logit[s][:, 0:1] - final[rows, 0:1]) / final[rows, 1:2]


def slope_body(kind, tok, grd, back, logit, final, out, dmix):
    centres = [jnp.zeros((32, 1), F32), jnp.zeros((32, 1), F32)]
    for s in range(4):
        top = pl.multiple_of(kind[s] * 32, 32)
        acc = jnp.zeros((32, 256), F32)
        for y in range(NY):
            for z in range(NL):
                d = slice(y * 1024 + z * 256, y * 1024 + z * 256 + 256)
                eo = back[y, z, pl.ds(top, 32), :].astype(F32)
                dm = back[y, z, pl.ds(top + 64, 32), :].astype(F32)
                acc = acc + (grd[s, :, d].astype(F32) * eo + tok[s, :, d].astype(F32) * dm)
        dm = jnp.sum(acc, axis=1, keepdims=True)
        dmix[s] = jnp.broadcast_to(dm, (32, 128))
        term = mix_of(kind, logit, final, s) * dm
        for k in range(2):
            centres[k] = centres[k] + jnp.where(kind[s] == k, term, 0.0)
    lane = lax.broadcasted_iota(jnp.int32, (8, 128), 1)
    tile = jnp.zeros((8, 128), F32)
    for k in range(2):
        for j in range(4):
            tile = jnp.where(lane == k * 4 + j, centres[k][j * 8 : j * 8 + 8], tile)
    for g in range(NL * NY):
        out[g] = tile


def final_body(kind, tok, back, logit, final, dmix, got, route, dtok, droute):
    tile = got[0]
    for g in range(1, NL * NY):
        tile = tile + got[g]
    centres = [
        jnp.concatenate([tile[:, k * 4 + j : k * 4 + j + 1] for j in range(4)], 0) for k in range(2)
    ]
    mixb, dlogit, tops = [], [], []
    for s in range(4):
        mix = mix_of(kind, logit, final, s)
        centre = jnp.where(kind[s] == 0, centres[0], centres[1])
        dlogit.append((mix * (dmix[s][:, 0:1] - centre)).astype(BF).astype(F32))
        mixb.append(mix.astype(BF).astype(F32))
        tops.append(pl.multiple_of(kind[s] * 32 + 64, 32))
    for y in range(NY):
        for z in range(NL):
            d = slice(y * 1024 + z * 256, y * 1024 + z * 256 + 256)
            r = route[:, d].astype(F32)
            acc = jnp.zeros((32, 256), F32)
            for s in range(4):
                dm = back[y, z, pl.ds(tops[s], 32), :].astype(F32)
                dtok[s, :, d] = (mixb[s] * dm + dlogit[s] * r).astype(BF)
                acc = acc + tok[s, :, d].astype(F32) * dlogit[s]
            total = jnp.sum(acc, axis=0, keepdims=True)
            i = (y * NL + z) // 2
            o = slice((z % 2) * 256, (z % 2) * 256 + 256)
            for g in range(16):
                droute[g, i : i + 1, o] = total


def shards(tokens, grad_out, members, router, w_in, w_out):
    def swap(value, axes):
        return lax.all_to_all(value, axes, split_axis=0, concat_axis=0, tiled=True)

    core = lax.axis_index("core")
    core_s = jnp.full((1,), core, jnp.int32)
    group = lax.axis_index(("zl", "y"))
    flip = [(a * 4 + b, b * 4 + a) for a in range(4) for b in range(4)]
    cores = [(0, 1), (1, 0)]

    route = router.reshape(1, 4096)

    sent, logit, kind = call(
        partial_body,
        [sds((NY, 144, 1024)), sds((4, 32, 128), F32), sds((4,), jnp.int32)],
        (route,),
        (jnp.full((1,), group * 4, jnp.int32), members),
        flops=10_000_000,
        any_args=(tokens, grad_out),
        scratch=(pltpu.VMEM((4, 32, 4096), BF), pltpu.VMEM((4, 32, 4096), BF), pltpu.SemaphoreType.DMA((8,))),
        limit=63 * 1024 * 1024,
    )
    shard = jnp.concatenate([w_in[0], w_out[0]], axis=0)
    shard = lax.ppermute(shard, ("x", "y"), flip)
    sent, shard = lax.optimization_barrier((sent, shard))
    shard = lax.all_gather(shard, "zh", axis=0, tiled=False)
    got = swap(sent, "y")
    got, shard = lax.optimization_barrier((got, shard))

    low = jnp.full((1,), lax.axis_index("zl"), jnp.int32)
    parts = call(over_y_body, [sds((160, 256))] * NL, (got,), (low,), flops=1_000_000)
    parts, shard = lax.optimization_barrier((parts, shard))
    shard = swap(jnp.broadcast_to(shard[None], (NX, NH, 256, 128)), "x")
    parts = [parts[0]] + [
        lax.ppermute(parts[i], "zl", [(z, (z + i) % NL) for z in range(NL)]) for i in range(1, NL)
    ]
    shard, parts = lax.optimization_barrier((shard, parts))
    sent, final = call(
        over_zl_body, [sds((NL, 128, 256)), sds((64, 128), F32)], tuple(parts), flops=300_000
    )
    sent, shard = lax.optimization_barrier((sent, shard))
    mixed = swap(sent, "zl")
    other = lax.ppermute(shard, "core", cores)
    half = lax.dynamic_slice_in_dim(mixed, (1 - core) * 128, 128, axis=2)
    mixed_half = lax.dynamic_slice_in_dim(mixed, core * 128, 128, axis=2)
    mixed_other = lax.ppermute(half, "core", cores)

    sent = call(hidden_body, sds((NY, 128, 512)), (mixed, shard, other), (core_s,), flops=140_000_000)
    got, mixed_other = lax.optimization_barrier((swap(sent, "y"), mixed_other))
    sent, inner = call(
        expert_body,
        [sds((NL, 128, 256)), sds((128, 512))],
        (got, shard, other),
        (core_s,),
        flops=140_000_000,
    )
    inner_other = lax.ppermute(inner, "core", cores)
    grads = call(
        weight_grad_body,
        sds((NX, NH, 256, 128)),
        (mixed_half, mixed_other, inner, inner_other),
        flops=140_000_000,
    )
    got, grads = lax.optimization_barrier((swap(sent, "zl"), grads))
    grads = lax.psum_scatter(grads.reshape(NX * NH * 256, 128), "x", scatter_dimension=0, tiled=True)

    sent = call(sum_four_body, sds((NL, 128, 256)), (got,), flops=300_000)
    sent = swap(sent, "zl")
    back = swap(jnp.broadcast_to(sent[None], (NY, NL, 128, 256)), "y")
    sent, dmix = call(
        slope_body,
        [sds((16, 8, 128), F32), sds((4, 32, 128), F32)],
        (tokens, grad_out, back, logit, final),
        (kind,),
        flops=5_000_000,
    )
    sent, grads = lax.optimization_barrier((sent, grads))
    grads = lax.psum_scatter(grads, "zh", scatter_dimension=0, tiled=True)
    grad_tokens, droute = call(
        final_body,
        [sds((4, 32, 4096)), sds((16, 8, 512), F32)],
        (tokens, back, logit, final, dmix, swap(sent, ("zl", "y")), route),
        (kind,),
        flops=5_000_000,
    )
    droute = jnp.sum(swap(droute, ("x", "y")), axis=0)
    droute = droute + lax.ppermute(droute, "core", cores)
    droute, grads = lax.optimization_barrier((droute, grads))
    droute = lax.dynamic_slice_in_dim(droute, core * 4, 4, axis=0)
    droute = swap(jnp.broadcast_to(droute[None], (16, 4, 512)), ("zh", "zl"))
    grads = lax.ppermute(grads, ("x", "y"), flip)
    droute, grads = lax.optimization_barrier((droute, grads))
    droute = lax.all_gather(jnp.sum(droute, axis=0), "core", axis=0, tiled=True)
    return grad_tokens, grads[None, :128], grads[None, 128:], droute.reshape(4096, 1)


def solution(mesh):
    fine = Mesh(mesh.devices.reshape(NX, NH, NC, NL, NY), AXES)
    dp, group = ("x", "zh", "core"), ("zl", "y")
    return jax.shard_map(
        shards,
        mesh=fine,
        in_specs=(
            P(dp + group, None, None),
            P(dp + group, None, None),
            P(dp, None),
            P(),
            P(None, dp, group),
            P(None, group, dp),
        ),
        out_specs=(P(dp + group, None, None), P(None, dp, group), P(None, group, dp), P()),
        check_vma=False,
    )
```

```python
import jax
import jax.numpy as jnp
from jax import lax
from jax.experimental import pallas as pl
from jax.experimental.pallas import tpu as pltpu
from jax.sharding import Mesh, PartitionSpec as P

BF = jnp.bfloat16
F32 = jnp.float32
LOWEST = -1e30
NX, NH, NC, NL, NY = 4, 4, 2, 4, 4
AXES = ("x", "zh", "core", "zl", "y")
HERE, THERE = 32, 32
LIMIT = 32 * 1024 * 1024


def call(body, outs, vmem_args, smem_args=(), flops=0, any_args=(), scratch=(), limit=LIMIT):
    multi = isinstance(outs, (list, tuple))
    arrays = list(smem_args) + list(vmem_args) + list(any_args)
    nbytes = sum(a.size * a.dtype.itemsize for a in arrays)
    for o in outs if multi else [outs]:
        nbytes += o.size * o.dtype.itemsize
    vm = pl.BlockSpec(memory_space=pltpu.VMEM)
    sm = pl.BlockSpec(memory_space=pltpu.SMEM)
    return pl.pallas_call(
        body,
        out_shape=outs,
        in_specs=[sm] * len(smem_args) + [vm] * len(vmem_args) + [pl.BlockSpec(memory_space=pl.ANY)] * len(any_args),
        out_specs=[sm if o.dtype == jnp.int32 else vm for o in outs] if multi else vm,
        scratch_shapes=list(scratch),
        compiler_params=pltpu.CompilerParams(vmem_limit_bytes=limit),
        cost_estimate=pl.CostEstimate(flops=flops, bytes_accessed=nbytes, transcendentals=0),
    )(*arrays)


def sds(shape, dtype=BF):
    return jax.ShapeDtypeStruct(shape, dtype)


def three(value):
    a = value.astype(BF).astype(F32)
    b = (value - a).astype(BF).astype(F32)
    c = (value - a - b).astype(BF).astype(F32)
    return a, b, c


def pack_stats(top, total):
    lane = lax.broadcasted_iota(jnp.int32, (top.shape[0], 128), 1)
    out = jnp.zeros((top.shape[0], 128), F32)
    for i, term in enumerate(three(top) + three(total)):
        out = jnp.where(lane == i, term, out)
    return out.astype(BF)


def unpack_stats(packed):
    packed = packed.astype(F32)
    lanes = [packed[:, i : i + 1] for i in range(6)]
    return (lanes[0] + lanes[1]) + lanes[2], (lanes[3] + lanes[4]) + lanes[5]


def merge_stats(stats):
    top = stats[0][0]
    for m, _ in stats[1:]:
        top = jnp.maximum(top, m)
    factors = [jnp.exp(m - top) for m, _ in stats]
    total = factors[0] * stats[0][1]
    for f, (_, s) in zip(factors[1:], stats[1:]):
        total = total + f * s
    return top, factors, total


def partial_body(first, order, route, tok_hbm, grd_hbm, out, logit, kind_out, tok, grd, sems):
    loads = [pltpu.make_async_copy(tok_hbm.at[s], tok.at[s], sems.at[s]) for s in range(4)]
    loads += [pltpu.make_async_copy(grd_hbm.at[s], grd.at[s], sems.at[4 + s]) for s in range(4)]
    for load in loads:
        load.start()
    kind = []
    for s in range(4):
        hits = jnp.int32(0)
        for j in range(32, 64):
            hits = hits + (order[0, j] == first[0] + s).astype(jnp.int32)
        kind_out[s] = hits
        kind.append(hits)
    ls = []
    for s in range(4):
        loads[s].wait()
        acc = jnp.zeros((32, 512), F32)
        for j in range(8):
            d = slice(j * 512, j * 512 + 512)
            acc = acc + tok[s, :, d].astype(F32) * route[:, d].astype(F32)
        l = jnp.sum(acc, axis=1, keepdims=True)
        ls.append(l)
        logit[s] = jnp.broadcast_to(l, (32, 128))
    tops, sums, weights = [], [], []
    for k in range(2):
        top = jnp.full((32, 1), LOWEST, F32)
        for s in range(4):
            top = jnp.maximum(top, jnp.where(kind[s] == k, ls[s], LOWEST))
        ws = [jnp.where(kind[s] == k, jnp.exp(jnp.minimum(ls[s] - top, 0.0)), 0.0) for s in range(4)]
        tops.append(top)
        sums.append((ws[0] + ws[1]) + (ws[2] + ws[3]))
        weights.append(ws)
    stats = pack_stats(jnp.concatenate(tops, 0), jnp.concatenate(sums, 0))
    for s in range(4):
        loads[4 + s].wait()
    for y in range(NY):
        for j in range(4):
            out[y, 128:144, j * 128 : j * 128 + 128] = stats[j * 16 : j * 16 + 16]
        out[y, 128:144, 512:1024] = jnp.zeros((16, 512), BF)
        for h in range(4):
            d = slice(y * 1024 + h * 256, y * 1024 + h * 256 + 256)
            o = slice(h * 256, h * 256 + 256)
            for base, ref in ((0, tok), (64, grd)):
                vals = [ref[s, :, d].astype(F32) for s in range(4)]
                for k in range(2):
                    w = weights[k]
                    acc = (w[0] * vals[0] + w[1] * vals[1]) + (w[2] * vals[2] + w[3] * vals[3])
                    out[y, base + k * 32 : base + k * 32 + 32, o] = acc.astype(BF)


def over_y_body(at, got, *outs):
    stats = []
    for i in range(NY):
        rows = [got[i, 128:144, j * 128 : j * 128 + 128] for j in range(4)]
        stats.append(unpack_stats(jnp.concatenate(rows, 0)))
    top, factors, total = merge_stats(stats)
    packed = pack_stats(top, total)
    for step, out in enumerate(outs):
        d = pl.ds(pl.multiple_of(lax.rem(at[0] + step, NL) * 256, 256), 256)
        for j in range(2):
            out[128:160, j * 128 : j * 128 + 128] = packed[j * 32 : j * 32 + 32]
        for base in (0, 64):
            acc = factors[0] * got[0, base : base + 64, d].astype(F32)
            for i in range(1, NY):
                acc = acc + factors[i] * got[i, base : base + 64, d].astype(F32)
            out[base : base + 64, :] = acc.astype(BF)


def over_zl_body(*refs):
    got, out, final = refs[:NL], refs[NL], refs[NL + 1]
    stats = []
    for i in range(NL):
        rows = [got[i][128:160, j * 128 : j * 128 + 128] for j in range(2)]
        stats.append(unpack_stats(jnp.concatenate(rows, 0)))
    top, factors, total = merge_stats(stats)
    scale = 1.0 / total
    lane = lax.broadcasted_iota(jnp.int32, (64, 128), 1)
    final[...] = jnp.where(lane == 0, top, total)
    factors = [f * scale for f in factors]
    for base in (0, 64):
        acc = factors[0] * got[0][base : base + 64].astype(F32)
        for i in range(1, NL):
            acc = acc + factors[i] * got[i][base : base + 64].astype(F32)
        acc = acc.astype(BF)
        for z in range(NL):
            out[z, base : base + 64] = acc


def weight_blocks(core, own, other, h, c):
    mine = core == c
    ins = [jnp.where(mine, own[a, h, :128], other[a, h, :128]) for a in range(NX)]
    outs = [jnp.where(mine, own[a, h, 128:], other[a, h, 128:]) for a in range(NX)]
    return jnp.concatenate(ins, 1), jnp.concatenate(outs, 0)


def hidden_body(core, mixed, own, other, out):
    hid = jnp.zeros((64, 512), F32)
    dact = jnp.zeros((64, 512), F32)
    for h in range(NH):
        for c in range(NC):
            win, wout = weight_blocks(core[0], own, other, h, c)
            lanes = slice(c * 128, c * 128 + 128)
            hid = hid + jnp.dot(mixed[h, :64, lanes], win, preferred_element_type=F32)
            dact = dact + lax.dot_general(
                mixed[h, 64:, lanes], wout, (((1,), (1,)), ((), ())), preferred_element_type=F32
            )
    hid = hid.astype(BF)
    dact = dact.astype(BF)
    for y in range(NY):
        out[y, :64] = hid
        out[y, 64:] = dact


def expert_body(core, got, own, other, out, inner):
    hid = got[0, :64].astype(F32)
    dact = got[0, 64:].astype(F32)
    for i in range(1, NY):
        hid = hid + got[i, :64].astype(F32)
        dact = dact + got[i, 64:].astype(F32)
    sigma = jax.nn.sigmoid(hid)
    act = (hid * sigma).astype(BF)
    dpre = (dact * (sigma * (1.0 + hid * (1.0 - sigma)))).astype(BF)
    inner[:64] = act
    inner[64:] = dpre
    for h in range(NH):
        for c in range(NC):
            win, wout = weight_blocks(core[0], own, other, h, c)
            lanes = slice(c * 128, c * 128 + 128)
            out[h, :64, lanes] = jnp.dot(act, wout, preferred_element_type=F32).astype(BF)
            out[h, 64:, lanes] = lax.dot_general(
                dpre, win, (((1,), (1,)), ((), ())), preferred_element_type=F32
            ).astype(BF)


def weight_grad_body(mixed, mixed_other, inner, inner_other, out):
    act = jnp.concatenate([inner[:64], inner_other[:64]], 0)
    dpre = jnp.concatenate([inner[64:], inner_other[64:]], 0)
    for h in range(NH):
        mix = jnp.concatenate([mixed[h, :64], mixed_other[h, :64]], 0)
        dmo = jnp.concatenate([mixed[h, 64:], mixed_other[h, 64:]], 0)
        gin = lax.dot_general(mix, dpre, (((0,), (0,)), ((), ())), preferred_element_type=F32)
        gout = lax.dot_general(act, dmo, (((0,), (0,)), ((), ())), preferred_element_type=F32)
        for a in range(NX):
            out[a, h, :128] = gin[:, a * 128 : a * 128 + 128].astype(BF)
            out[a, h, 128:] = gout[a * 128 : a * 128 + 128].astype(BF)


def sum_four_body(got, out):
    acc = got[0].astype(F32)
    for i in range(1, NL):
        acc = acc + got[i].astype(F32)
    acc = acc.astype(BF)
    for z in range(NL):
        out[z] = acc


def mix_of(kind, logit, final, s):
    rows = pl.ds(pl.multiple_of(kind[s] * 32, 32), 32)
    return jnp.exp(logit[s][:, 0:1] - final[rows, 0:1]) / final[rows, 1:2]


def slope_body(kind, tok, grd, back, logit, final, out, dmix):
    centres = [jnp.zeros((32, 1), F32), jnp.zeros((32, 1), F32)]
    for s in range(4):
        top = pl.multiple_of(kind[s] * 32, 32)
        acc = jnp.zeros((32, 256), F32)
        for y in range(NY):
            for z in range(NL):
                d = slice(y * 1024 + z * 256, y * 1024 + z * 256 + 256)
                eo = back[y, z, pl.ds(top, 32), :].astype(F32)
                dm = back[y, z, pl.ds(top + 64, 32), :].astype(F32)
                acc = acc + (grd[s, :, d].astype(F32) * eo + tok[s, :, d].astype(F32) * dm)
        dm = jnp.sum(acc, axis=1, keepdims=True)
        dmix[s] = jnp.broadcast_to(dm, (32, 128))
        term = mix_of(kind, logit, final, s) * dm
        for k in range(2):
            centres[k] = centres[k] + jnp.where(kind[s] == k, term, 0.0)
    lane = lax.broadcasted_iota(jnp.int32, (8, 128), 1)
    tile = jnp.zeros((8, 128), F32)
    for k in range(2):
        for j in range(4):
            tile = jnp.where(lane == k * 4 + j, centres[k][j * 8 : j * 8 + 8], tile)
    for g in range(NL * NY):
        out[g] = tile


def final_body(kind, tok, back, logit, final, dmix, got, route, dtok, droute):
    tile = got[0]
    for g in range(1, NL * NY):
        tile = tile + got[g]
    centres = [
        jnp.concatenate([tile[:, k * 4 + j : k * 4 + j + 1] for j in range(4)], 0) for k in range(2)
    ]
    mixb, dlogit, tops = [], [], []
    for s in range(4):
        mix = mix_of(kind, logit, final, s)
        centre = jnp.where(kind[s] == 0, centres[0], centres[1])
        dlogit.append((mix * (dmix[s][:, 0:1] - centre)).astype(BF).astype(F32))
        mixb.append(mix.astype(BF).astype(F32))
        tops.append(pl.multiple_of(kind[s] * 32 + 64, 32))
    for y in range(NY):
        for z in range(NL):
            d = slice(y * 1024 + z * 256, y * 1024 + z * 256 + 256)
            r = route[:, d].astype(F32)
            acc = jnp.zeros((32, 256), F32)
            for s in range(4):
                dm = back[y, z, pl.ds(tops[s], 32), :].astype(F32)
                dtok[s, :, d] = (mixb[s] * dm + dlogit[s] * r).astype(BF)
                acc = acc + tok[s, :, d].astype(F32) * dlogit[s]
            total = jnp.sum(acc, axis=0, keepdims=True)
            i = (y * NL + z) // 2
            o = slice((z % 2) * 256, (z % 2) * 256 + 256)
            for g in range(16):
                droute[g, i : i + 1, o] = total


def shards(tokens, grad_out, members, router, w_in, w_out):
    def swap(value, axes):
        return lax.all_to_all(value, axes, split_axis=0, concat_axis=0, tiled=True)

    core = lax.axis_index("core")
    core_s = jnp.full((1,), core, jnp.int32)
    group = lax.axis_index(("zl", "y"))
    flip = [(a * 4 + b, b * 4 + a) for a in range(4) for b in range(4)]
    cores = [(0, 1), (1, 0)]

    route = router.reshape(1, 4096)

    sent, logit, kind = call(
        partial_body,
        [sds((NY, 144, 1024)), sds((4, 32, 128), F32), sds((4,), jnp.int32)],
        (route,),
        (jnp.full((1,), group * 4, jnp.int32), members),
        flops=10_000_000,
        any_args=(tokens, grad_out),
        scratch=(pltpu.VMEM((4, 32, 4096), BF), pltpu.VMEM((4, 32, 4096), BF), pltpu.SemaphoreType.DMA((8,))),
        limit=63 * 1024 * 1024,
    )
    shard = jnp.concatenate([w_in[0], w_out[0]], axis=0)
    shard = lax.ppermute(shard, ("x", "y"), flip)
    sent, shard = lax.optimization_barrier((sent, shard))
    shard = lax.all_gather(shard, "zh", axis=0, tiled=False)
    got = swap(sent, "y")
    got, shard = lax.optimization_barrier((got, shard))

    low = jnp.full((1,), lax.axis_index("zl"), jnp.int32)
    parts = call(over_y_body, [sds((160, 256))] * NL, (got,), (low,), flops=1_000_000)
    parts, shard = lax.optimization_barrier((parts, shard))
    shard = swap(jnp.broadcast_to(shard[None], (NX, NH, 256, 128)), "x")
    parts = [parts[0]] + [
        lax.ppermute(parts[i], "zl", [(z, (z + i) % NL) for z in range(NL)]) for i in range(1, NL)
    ]
    shard, parts = lax.optimization_barrier((shard, parts))
    sent, final = call(
        over_zl_body, [sds((NL, 128, 256)), sds((64, 128), F32)], tuple(parts), flops=300_000
    )
    sent, shard = lax.optimization_barrier((sent, shard))
    mixed = swap(sent, "zl")
    other = lax.ppermute(shard, "core", cores)
    half = lax.dynamic_slice_in_dim(mixed, (1 - core) * 128, 128, axis=2)
    mixed_half = lax.dynamic_slice_in_dim(mixed, core * 128, 128, axis=2)
    mixed_other = lax.ppermute(half, "core", cores)

    sent = call(hidden_body, sds((NY, 128, 512)), (mixed, shard, other), (core_s,), flops=140_000_000)
    got, mixed_other = lax.optimization_barrier((swap(sent, "y"), mixed_other))
    sent, inner = call(
        expert_body,
        [sds((NL, 128, 256)), sds((128, 512))],
        (got, shard, other),
        (core_s,),
        flops=140_000_000,
    )
    inner_other = lax.ppermute(inner, "core", cores)
    grads = call(
        weight_grad_body,
        sds((NX, NH, 256, 128)),
        (mixed_half, mixed_other, inner, inner_other),
        flops=140_000_000,
    )
    got, grads = lax.optimization_barrier((swap(sent, "zl"), grads))
    grads = lax.psum_scatter(grads.reshape(NX * NH * 256, 128), "x", scatter_dimension=0, tiled=True)

    sent = call(sum_four_body, sds((NL, 128, 256)), (got,), flops=300_000)
    sent = swap(sent, "zl")
    back = swap(jnp.broadcast_to(sent[None], (NY, NL, 128, 256)), "y")
    back, grads = lax.optimization_barrier((back, grads))
    grads = lax.psum_scatter(grads, "zh", scatter_dimension=0, tiled=True)
    sent, dmix = call(
        slope_body,
        [sds((16, 8, 128), F32), sds((4, 32, 128), F32)],
        (tokens, grad_out, back, logit, final),
        (kind,),
        flops=5_000_000,
    )
    grad_tokens, droute = call(
        final_body,
        [sds((4, 32, 4096)), sds((16, 8, 512), F32)],
        (tokens, back, logit, final, dmix, swap(sent, ("zl", "y")), route),
        (kind,),
        flops=5_000_000,
    )
    droute = jnp.sum(swap(droute, ("x", "y")), axis=0)
    droute = droute + lax.ppermute(droute, "core", cores)
    droute, grads = lax.optimization_barrier((droute, grads))
    droute = lax.dynamic_slice_in_dim(droute, core * 4, 4, axis=0)
    droute = swap(jnp.broadcast_to(droute[None], (16, 4, 512)), ("zh", "zl"))
    grads = lax.ppermute(grads, ("x", "y"), flip)
    droute, grads = lax.optimization_barrier((droute, grads))
    droute = lax.all_gather(jnp.sum(droute, axis=0), "core", axis=0, tiled=True)
    return grad_tokens, grads[None, :128], grads[None, 128:], droute.reshape(4096, 1)


def solution(mesh):
    fine = Mesh(mesh.devices.reshape(NX, NH, NC, NL, NY), AXES)
    dp, group = ("x", "zh", "core"), ("zl", "y")
    return jax.shard_map(
        shards,
        mesh=fine,
        in_specs=(
            P(dp + group, None, None),
            P(dp + group, None, None),
            P(dp, None),
            P(),
            P(None, dp, group),
            P(None, group, dp),
        ),
        out_specs=(P(dp + group, None, None), P(None, dp, group), P(None, group, dp), P()),
        check_vma=False,
    )
```
